32 devices in a mesh: group: 4 (over y, core), member: 8 (over z, x).
Axes of the slice: x: 2, y: 2, z: 4, core: 2. Of those that a mesh axis runs over, the one named last changes fastest.
Arguments:
- queries: bfloat16 [256, 32, 128], P('group'), may hold values from -0.5 to 0.5
- centroids: bfloat16 [131072, 128], P('member'), may hold values from -0.5 to 0.5
- doc_resid: bfloat16 [8192, 128, 128], P(('group', 'member')), may hold values from -6 to 6
- doc_codes: int32 [8192, 128], P(('group', 'member')), may hold values from 0 to 131071
- doc_scale: bfloat16 [8192], P(('group', 'member')), may hold values from 0.019897461 to 0.19921875
- doc_len: int32 [8192], P(('group', 'member')), may hold values from 1 to 128
- send_list: int32 [32, 32, 2], P(('group', 'member')), may hold values from 0 to 255
- cand: int32 [256, 1024], P('group', 'member'), may hold values from 0 to 63
Outputs:
- scores: float32 [256, 1024], P('group', 'member')
The draws below stay inside these ranges and needn't reach their ends.
Inputs may be any that keep to these rules, and one draw needn't show every extreme that they name: `cand`: slot s names the document source s div 2 sent to this candidate's device in its slot s mod 2.
All inputs are finite; a program needn't handle non-finite values.
Results may differ from the reference program's by a relative error of at most 0.0003.
Values may be sent and summed in bfloat16 or wider, within the bound.
A program may use at most 256 MiB of HBM per device.

```python
import math
import jax
import jax.numpy as jnp
import numpy as np
from jax import lax

DIM = 128
QT = 32
BLK = 128
CENT = 131072
QG = 64
DOCS_DEV = 256
CAP = 2
KM = 128
QUERIES = 256
K = 1024
DOCS = 8192
N_MEMBER = 8
DEVICES = 32


def plant(array, rng, low, top_value):
    longest = array.shape.index(max(array.shape))
    spots = []
    for shift in (0, 1):
        where = [jax.random.randint(jax.random.fold_in(rng, axis), (), 0, length) for axis, length in enumerate(array.shape)]
        where[longest] = (where[longest] + shift) % array.shape[longest]
        spots.append(tuple(where))
    return array.at[spots[0]].set(low).at[spots[1]].set(top_value)


def block_scale(rng, shape, pieces, smallest, top_value):
    level, own = 1.0, jax.random.fold_in(rng, 6)
    for dim, shards_of in pieces:
        heights = jnp.exp(jax.random.uniform(jax.random.fold_in(own, dim), (shards_of,), jnp.float32, smallest / len(pieces), top_value / len(pieces)))
        level = level * jnp.repeat(heights, shape[dim] // shards_of).reshape([-1 if axis == dim else 1 for axis in range(len(shape))])
    return level


def wide_ids(key, extent, count, slope):
    portions = [min(1 << octave, count + 1 - (1 << octave)) * (1 << 20) // math.isqrt((1 << octave) ** slope) + 1 for octave in range((count + 1).bit_length()) if 1 << octave <= count]
    scale = 1 + sum(portions) // (1 << 30)
    table = np.cumsum(np.array([max(1, weight // scale) for weight in portions]))
    pick = jax.random.randint(jax.random.fold_in(key, 1), extent, 0, int(table[len(portions) - 1]))
    start = jnp.left_shift(1, jnp.searchsorted(jnp.asarray(table, jnp.int32), pick, side="right").astype(jnp.int32))
    grade = start - 1 + jax.random.randint(jax.random.fold_in(key, 4), extent, 0, 1 << 30) % jnp.minimum(start, count + 1 - start)
    return jax.random.permutation(jax.random.fold_in(key, 2), count)[grade].astype(jnp.int32)


def scatter_about(stream_key, shape, scale, limit, pieces=(), held_as=jnp.bfloat16):
    result = scale * jax.random.normal(stream_key, shape, jnp.float32)
    if pieces:
        result = result * block_scale(stream_key, shape, pieces, -0.22, 0.18)
    return jnp.clip(result, -limit, limit).astype(held_as)


def setup_inputs(seed: int = 0) -> dict:
    streams_of = jax.random.split(jax.random.key(seed), 9)
    return {
        "queries": scatter_about(streams_of[0], (QUERIES, QT, DIM), DIM ** -0.5, 0.5, ((0, 4),)),
        "centroids": scatter_about(streams_of[1], (CENT, DIM), DIM ** -0.5, 0.5, ((0, 8),)),
        "doc_resid": scatter_about(streams_of[2], (DOCS, BLK, DIM), 1.0, 6.0, ((0, 32),)),
        "doc_codes": plant(wide_ids(streams_of[3], (DOCS, BLK), CENT, 2), jax.random.fold_in(streams_of[3], 3), 0, CENT - 1).astype(jnp.int32),
        "doc_scale": jnp.clip(jnp.exp(math.log(0.19921875) - 2.3038113 * jax.random.uniform(streams_of[4], (DOCS,), jnp.float32) ** block_scale(streams_of[4], (DOCS,), ((0, 32),), -0.2, 0.2)), 0.019897461, 0.19921875).astype(jnp.bfloat16),
        "doc_len": plant(jax.random.randint(streams_of[5], (DOCS,), 1, BLK + 1), jax.random.fold_in(streams_of[5], 1), 1, BLK).astype(jnp.int32),
        "send_list": plant(jax.random.randint(streams_of[6], (DEVICES, DEVICES, CAP), 0, DOCS_DEV), jax.random.fold_in(streams_of[6], 1), 0, DOCS_DEV - 1).astype(jnp.int32),
        "cand": plant(jax.random.randint(streams_of[7], (QUERIES, K), 0, DEVICES * CAP), jax.random.fold_in(streams_of[7], 1), 0, (DEVICES * CAP) - 1).astype(jnp.int32),
    }


def reference(queries, centroids, doc_resid, doc_codes, doc_scale, doc_len, send_list, cand):
    query_group = (jnp.arange(QUERIES, dtype=jnp.int32) // QG)[:, None]
    member_index = (jnp.arange(K, dtype=jnp.int32) // KM)[None, :]
    destination = (query_group * N_MEMBER + member_index).astype(jnp.int32)
    source = (cand // CAP).astype(jnp.int32)
    column = (cand % CAP).astype(jnp.int32)
    doc_index = (source * DOCS_DEV + send_list[source, destination, column]).astype(jnp.int32)

    def one_query(items):
        query, docs = items
        codes = doc_codes[docs]
        embedding = (centroids[codes].astype(jnp.float32)
                     + doc_scale[docs].astype(jnp.float32)[:, None, None] * doc_resid[docs].astype(jnp.float32)).astype(jnp.bfloat16)
        sims = jnp.einsum("td,kjd->ktj", query.astype(jnp.float32), embedding.astype(jnp.float32))
        valid = jnp.arange(BLK, dtype=jnp.int32)[None, :] < doc_len[docs][:, None]
        sims = jnp.where(valid[:, None, :], sims, jnp.float32(-1.0e9))
        return jnp.mean(jnp.max(sims, axis=2), axis=1)

    return lax.map(one_query, (queries, doc_index))
```

```python
import functools

import jax
import jax.numpy as jnp
from jax import lax
from jax.experimental import pallas as pl
from jax.experimental.pallas import tpu as pltpu
from jax.sharding import PartitionSpec as P

LANES = 128
PAD = 8
VMEM_LIMIT = 56 * 1024 * 1024


def widen(source, wide, offset, rows):
    step = 256

    @pl.loop(0, rows // step)
    def _(i):
        at = pl.multiple_of(i * step, step)
        wide[pl.ds(at + offset, step), :] = source[pl.ds(at, step), :].astype(jnp.float32)


def fetch_kernel(entries, table, out, wide, stage):
    rows = table.shape[0]
    widen(table, wide, PAD, rows)
    block = stage.shape[0]

    @pl.loop(0, out.shape[0] // block)
    def _(b):
        at = pl.multiple_of(b * block, block)

        @pl.when(entries[at] > 0)
        def _():
            for u in range(block):
                stage[pl.ds(u, 1), :] = wide[pl.ds(entries[at + u], 1), :]
            out[pl.ds(at, block), :] = stage[...].astype(out.dtype)


def fetch_rows(entries, table):
    count, (rows, width) = entries.shape[0], table.shape
    return pl.pallas_call(
        fetch_kernel,
        out_shape=jax.ShapeDtypeStruct((count, width), table.dtype),
        grid_spec=pltpu.PrefetchScalarGridSpec(
            num_scalar_prefetch=1,
            grid=(1,),
            in_specs=[pl.BlockSpec((rows, width), lambda i, e: (0, 0))],
            out_specs=pl.BlockSpec((count, width), lambda i, e: (0, 0)),
            scratch_shapes=[
                pltpu.VMEM((rows + PAD, width), jnp.float32),
                pltpu.VMEM((LANES, width), jnp.float32),
            ],
        ),
        compiler_params=pltpu.CompilerParams(vmem_limit_bytes=VMEM_LIMIT),
    )(entries, table)


def score_kernel(docs, qtokens, chosen, place, lengths, scales, received, *refs):
    residuals, (queries, out, wide, stage, embedded) = refs[:docs], refs[docs:]
    step = pl.program_id(0)
    block, width = stage.shape
    tile = 16

    @pl.when(step == 0)
    def _():
        widen(received, wide, 0, received.shape[0])

    slot = lax.broadcasted_iota(jnp.int32, (block, width), 0)
    for k in range(docs):
        doc = step * docs + k
        length = lengths[doc]
        base = doc * block
        for first in range(0, block, tile):

            @pl.when(first < length)
            def _():
                for u in range(first, first + tile):
                    stage[pl.ds(u, 1), :] = wide[pl.ds(place[base + u], 1), :]

        value = stage[...] + scales[doc] * residuals[k][0].astype(jnp.float32)
        value = jnp.where(slot < length, value, value[0:1, :])
        embedded[pl.ds(k * block, block), :] = value.astype(embedded.dtype)

    chunk = out.shape[1]
    total = jnp.zeros(out.shape, jnp.float32)
    for first in range(0, queries.shape[2], chunk):
        sims = jnp.dot(
            embedded[...],
            queries[0, :, first : first + chunk],
            preferred_element_type=jnp.float32,
        )
        total = total + jnp.max(sims.reshape(docs, block, chunk), axis=1)
    out[...] = total * (1.0 / qtokens)


def score(chosen, place, lengths, scales, received, doc_resid, queries, qcount):
    slots = chosen.shape[0]
    block, width = doc_resid.shape[1:]
    groups, _, columns = queries.shape
    docs = 8
    per_group = slots // groups
    chunk = max(256, qcount)

    def residual_spec(k):
        return pl.BlockSpec(
            (1, block, width), lambda i, chosen, *_: (chosen[i * docs + k], 0, 0)
        )

    out = pl.pallas_call(
        functools.partial(score_kernel, docs, columns // qcount),
        out_shape=jax.ShapeDtypeStruct((slots, chunk), jnp.float32),
        grid_spec=pltpu.PrefetchScalarGridSpec(
            num_scalar_prefetch=4,
            grid=(slots // docs,),
            in_specs=[pl.BlockSpec(received.shape, lambda i, *_: (0, 0))]
            + [residual_spec(k) for k in range(docs)]
            + [
                pl.BlockSpec(
                    (1, width, columns), lambda i, *_: (i * docs // per_group, 0, 0)
                )
            ],
            out_specs=pl.BlockSpec((docs, chunk), lambda i, *_: (i, 0)),
            scratch_shapes=[
                pltpu.VMEM(received.shape, jnp.float32),
                pltpu.VMEM((block, width), jnp.float32),
                pltpu.VMEM((docs * block, width), jnp.bfloat16),
            ],
        ),
        compiler_params=pltpu.CompilerParams(vmem_limit_bytes=VMEM_LIMIT),
    )(chosen, place, lengths, scales, received, *([doc_resid] * docs), queries)
    return out.reshape(slots, chunk // qcount, qcount).sum(axis=1)


def make_lists(codes, valid, members, shard, capacity):
    rows, block = codes.shape
    owner = codes // shard
    needed = (owner[None] == jnp.arange(members)[:, None, None]) & valid[None]
    marks = needed.astype(jnp.bfloat16)
    earlier = jnp.triu(jnp.ones((block, block), jnp.bfloat16), 1)
    inside = jnp.einsum("orj,jk->ork", marks, earlier, preferred_element_type=jnp.float32)
    counts = jnp.sum(marks.astype(jnp.float32), axis=2)
    before = jnp.einsum(
        "or,rs->os",
        counts.astype(jnp.bfloat16),
        jnp.triu(jnp.ones((rows, rows), jnp.bfloat16), 1),
        preferred_element_type=jnp.float32,
    )
    position = jnp.sum(jnp.where(needed, inside + before[:, :, None], 0.0), axis=0)
    position = position.astype(jnp.int32)
    overflow = jnp.max(jnp.sum(counts, axis=1)).astype(jnp.int32) > capacity
    held = valid & (position < capacity)
    place = jnp.where(held, owner * capacity + position, 0)
    entry = codes - owner * shard + PAD
    lines = members * capacity // LANES
    line = jnp.where(held, place // LANES, -1).reshape(1, -1)
    low, high = (entry % 256).reshape(1, -1), (entry // 256).reshape(1, -1)
    on_line = line == jnp.arange(lines)[:, None]
    left = jnp.concatenate(
        [jnp.where(on_line, low, 0), jnp.where(on_line, high, 0)], axis=0
    ).astype(jnp.bfloat16)
    right = (place.reshape(1, -1) % LANES == jnp.arange(LANES)[:, None]).astype(jnp.bfloat16)
    packed = jnp.einsum("fi,gi->fg", left, right, preferred_element_type=jnp.float32)
    packed = packed.astype(jnp.int32)
    lists = packed[:lines] + 256 * packed[lines:]
    return lists.reshape(members, capacity), place, overflow


def body(queries, centroids, doc_resid, doc_codes, doc_scale, doc_len, send_list, cand):
    groups = lax.axis_size("group")
    members = lax.axis_size("member")
    capacity_sent = send_list.shape[2]
    block, width = doc_resid.shape[1:]
    shard = centroids.shape[0]
    qcount, qtokens = queries.shape[:2]

    chosen = send_list[0].reshape(-1)
    slots = chosen.shape[0]
    codes = jnp.take(doc_codes, chosen, axis=0)
    scales = jnp.take(doc_scale, chosen, axis=0).astype(jnp.float32)
    lengths = jnp.take(doc_len, chosen, axis=0)
    valid = jnp.arange(block, dtype=jnp.int32)[None, :] < lengths[:, None]

    lookups = slots * block
    capacity = -(-lookups // (members * LANES)) * LANES
    lists, place, overflow = make_lists(codes, valid, members, shard, capacity)
    flag = jnp.broadcast_to(overflow.astype(jnp.int32), (members, LANES))
    asked = lax.all_to_all(
        jnp.concatenate([lists, flag], axis=1), "member", split_axis=0, concat_axis=0, tiled=True
    )
    overflow = jnp.max(asked[:, capacity:]) > 0
    rows = fetch_rows(asked[:, :capacity].reshape(-1), centroids)
    received = lax.all_to_all(rows, "member", split_axis=0, concat_axis=0, tiled=True)

    turned = queries.transpose(2, 1, 0).reshape(width, qtokens * qcount)
    every_query = lax.all_gather(turned, "group", axis=0)

    def listed():
        return score(
            chosen, place.reshape(-1), lengths, scales, received, doc_resid, every_query, qcount
        )

    def whole_table():
        table = lax.all_gather(centroids, "member", axis=0, tiled=True)
        base = jnp.take(table, codes.reshape(-1), axis=0)
        own = jnp.arange(lookups, dtype=jnp.int32)
        return score(chosen, own, lengths, scales, base, doc_resid, every_query, qcount)

    local = lax.cond(overflow, whole_table, listed)
    local = local.reshape(groups * members, capacity_sent, qcount)
    returned = lax.all_to_all(local, ("group", "member"), split_axis=0, concat_axis=0, tiled=True)
    dense = returned.reshape(-1, qcount).T
    hit = cand[:, :, None] == jnp.arange(dense.shape[1], dtype=jnp.int32)
    return jnp.sum(jnp.where(hit, dense[:, None, :], 0.0), axis=2)


def solution(mesh):
    placed = (
        P("group", None, None),
        P("member", None),
        P(("group", "member"), None, None),
        P(("group", "member"), None),
        P(("group", "member")),
        P(("group", "member")),
        P(("group", "member"), None, None),
        P("group", "member"),
    )
    return jax.shard_map(
        body, mesh=mesh, in_specs=placed, out_specs=P("group", "member"), check_vma=False
    )
```

```python
import functools

import jax
import jax.numpy as jnp
from jax import lax
from jax.experimental import pallas as pl
from jax.experimental.pallas import tpu as pltpu
from jax.sharding import PartitionSpec as P

LANES = 128
PAD = 8
VMEM_LIMIT = 56 * 1024 * 1024


def widen(source, wide, offset, rows):
    step = 256

    @pl.loop(0, rows // step)
    def _(i):
        at = pl.multiple_of(i * step, step)
        wide[pl.ds(at + offset, step), :] = source[pl.ds(at, step), :].astype(jnp.float32)


def fetch_kernel(entries, table, out, wide, stage):
    rows = table.shape[0]
    widen(table, wide, PAD, rows)
    block = stage.shape[0]

    @pl.loop(0, out.shape[0] // block)
    def _(b):
        at = pl.multiple_of(b * block, block)

        @pl.when(entries[at] > 0)
        def _():
            for u in range(block):
                stage[pl.ds(u, 1), :] = wide[pl.ds(entries[at + u], 1), :]
            out[pl.ds(at, block), :] = stage[...].astype(out.dtype)


def fetch_rows(entries, table):
    count, (rows, width) = entries.shape[0], table.shape
    return pl.pallas_call(
        fetch_kernel,
        out_shape=jax.ShapeDtypeStruct((count, width), table.dtype),
        grid_spec=pltpu.PrefetchScalarGridSpec(
            num_scalar_prefetch=1,
            grid=(1,),
            in_specs=[pl.BlockSpec((rows, width), lambda i, e: (0, 0))],
            out_specs=pl.BlockSpec((count, width), lambda i, e: (0, 0)),
            scratch_shapes=[
                pltpu.VMEM((rows + PAD, width), jnp.float32),
                pltpu.VMEM((LANES, width), jnp.float32),
            ],
        ),
        compiler_params=pltpu.CompilerParams(vmem_limit_bytes=VMEM_LIMIT),
    )(entries, table)


def score_kernel(docs, qtokens, chosen, place, lengths, scales, holder, received, *refs):
    residuals, (queries, out, wide, stage, embedded) = refs[:docs], refs[docs:]
    step = pl.program_id(0)
    block, width = stage.shape
    tile = 16

    @pl.when(step == 0)
    def _():
        widen(received, wide, 0, received.shape[0])

    slot = lax.broadcasted_iota(jnp.int32, (block, width), 0)
    for k in range(docs):
        doc = step * docs + k
        length = lengths[doc]
        base = doc * block
        for first in range(0, block, tile):

            @pl.when(first < length)
            def _():
                for u in range(first, first + tile):
                    stage[pl.ds(u, 1), :] = wide[pl.ds(place[base + u], 1), :]

        value = stage[...] + scales[doc] * residuals[k][0].astype(jnp.float32)
        value = jnp.where(slot < length, value, value[0:1, :])
        embedded[pl.ds(k * block, block), :] = value.astype(embedded.dtype)

    chunk = out.shape[1]
    total = jnp.zeros(out.shape, jnp.float32)
    for first in range(0, queries.shape[2], chunk):
        sims = jnp.dot(
            embedded[...],
            queries[0, :, first : first + chunk],
            preferred_element_type=jnp.float32,
        )
        total = total + jnp.max(sims.reshape(docs, block, chunk), axis=1)
    out[...] = total * (1.0 / qtokens)


def score(chosen, place, lengths, scales, holder, received, doc_resid, queries, qcount):
    slots = chosen.shape[0]
    block, width = doc_resid.shape[1:]
    groups, _, columns = queries.shape
    docs = 8
    per_group = slots // groups
    chunk = max(256, qcount)

    def residual_spec(k):
        return pl.BlockSpec(
            (1, block, width), lambda i, chosen, *_: (chosen[i * docs + k], 0, 0)
        )

    out = pl.pallas_call(
        functools.partial(score_kernel, docs, columns // qcount),
        out_shape=jax.ShapeDtypeStruct((slots, chunk), jnp.float32),
        grid_spec=pltpu.PrefetchScalarGridSpec(
            num_scalar_prefetch=5,
            grid=(slots // docs,),
            in_specs=[pl.BlockSpec(received.shape, lambda i, *_: (0, 0))]
            + [residual_spec(k) for k in range(docs)]
            + [
                pl.BlockSpec(
                    (1, width, columns),
                    lambda i, chosen, place, lengths, scales, holder, *_: (
                        holder[i * docs // per_group],
                        0,
                        0,
                    ),
                )
            ],
            out_specs=pl.BlockSpec((docs, chunk), lambda i, *_: (i, 0)),
            scratch_shapes=[
                pltpu.VMEM(received.shape, jnp.float32),
                pltpu.VMEM((block, width), jnp.float32),
                pltpu.VMEM((docs * block, width), jnp.bfloat16),
            ],
        ),
        compiler_params=pltpu.CompilerParams(vmem_limit_bytes=VMEM_LIMIT),
    )(chosen, place, lengths, scales, holder, received, *([doc_resid] * docs), queries)
    return out.reshape(slots, chunk // qcount, qcount).sum(axis=1)


def pack_kernel(members, capacity, codes, place, lists, highest, seen, ranks, sums):
    steps, span = codes.shape
    lines = seen.shape[0]
    part = lines // members
    shard = part * LANES
    stripe = min(256, lines)
    list_lines = lists.shape[0]

    def same(count, row, first=0):
        found = lax.broadcasted_iota(jnp.int32, (count, span), 0) + first == row
        return jnp.where(found, 1.0, 0.0).astype(jnp.bfloat16)

    def across(left, right):
        return lax.dot_general(
            left, right, (((1,), (1,)), ((), ())), preferred_element_type=jnp.float32
        )

    seen[...] = jnp.zeros_like(seen)
    sums[...] = jnp.zeros_like(sums)

    @pl.loop(0, steps)
    def _(i):
        code = codes[pl.ds(i, 1), :]
        line, lane = code >> 7, code & (LANES - 1)
        right = same(LANES, lane)
        for first in range(0, lines, stripe):
            seen[first : first + stripe, :] += across(same(stripe, line, first), right)

    square = (LANES, LANES)
    earlier_lane = lax.broadcasted_iota(jnp.int32, square, 0) < lax.broadcasted_iota(
        jnp.int32, square, 1
    )
    earlier_lane = jnp.where(earlier_lane, 1.0, 0.0).astype(jnp.bfloat16)
    every_lane = jnp.ones(square, jnp.bfloat16)
    square = (part, part)
    earlier_line = lax.broadcasted_iota(jnp.int32, square, 1) < lax.broadcasted_iota(
        jnp.int32, square, 0
    )
    earlier_line = jnp.where(earlier_line, 1.0, 0.0).astype(jnp.bfloat16)
    top = jnp.zeros((1, LANES), jnp.float32)
    for o in range(members):
        at = slice(o * part, (o + 1) * part)
        present = jnp.where(seen[at, :] > 0.0, 1.0, 0.0)
        marks = present.astype(jnp.bfloat16)
        above = jnp.dot(earlier_line, marks, preferred_element_type=jnp.float32)
        rank = jnp.dot(marks, earlier_lane, preferred_element_type=jnp.float32) + jnp.dot(
            above.astype(jnp.bfloat16), every_lane, preferred_element_type=jnp.float32
        )
        top = jnp.maximum(top, jnp.max(present * (rank + 1.0), axis=0, keepdims=True))
        coarse = jnp.floor(rank * (1.0 / LANES))
        fine = rank - coarse * LANES
        ranks[0:LANES, at] = coarse.T.astype(jnp.bfloat16)
        ranks[LANES : 2 * LANES, at] = fine.T.astype(jnp.bfloat16)
    highest[...] = jnp.broadcast_to(top, highest.shape)

    @pl.loop(0, steps)
    def _(i):
        code = codes[pl.ds(i, 1), :]
        line, lane = code >> 7, code & (LANES - 1)
        found = jnp.zeros((2 * LANES, span), jnp.float32)
        for first in range(0, lines, stripe):
            found += jnp.dot(
                ranks[:, first : first + stripe],
                same(stripe, line, first),
                preferred_element_type=jnp.float32,
            )
        mine = lax.broadcasted_iota(jnp.int32, (LANES, span), 0) == lane
        pick = jnp.where(mine, found[:LANES] * LANES + found[LANES:], 0.0)
        rank = jnp.sum(pick, axis=0, keepdims=True).astype(jnp.int32)
        held = (code >= 0) & (rank < capacity)
        owner = jnp.maximum(line, 0) // part
        spot = jnp.where(held, owner * capacity + rank, 0)
        place[pl.ds(i, 1), :] = spot
        entry = code - owner * shard + PAD
        mark = same(list_lines, jnp.where(held, spot >> 7, -1)).astype(jnp.float32)
        left = jnp.concatenate(
            [
                mark * (entry & 255).astype(jnp.float32),
                mark * (entry >> 8).astype(jnp.float32),
                mark,
            ],
            axis=0,
        )
        sums[...] += across(left.astype(jnp.bfloat16), same(LANES, spot & (LANES - 1)))

    times = jnp.maximum(sums[2 * list_lines :, :], 1.0)
    low = (sums[:list_lines, :] / times + 0.5).astype(jnp.int32)
    high = (sums[list_lines : 2 * list_lines, :] / times + 0.5).astype(jnp.int32)
    lists[...] = low + 256 * high


def make_lists(wanted, members, shard, capacity):
    span = 256
    steps = wanted.size // span
    lines = members * shard // LANES
    list_lines = members * capacity // LANES
    place, lists, highest = pl.pallas_call(
        functools.partial(pack_kernel, members, capacity),
        out_shape=(
            jax.ShapeDtypeStruct((steps, span), jnp.int32),
            jax.ShapeDtypeStruct((list_lines, LANES), jnp.int32),
            jax.ShapeDtypeStruct((8, LANES), jnp.float32),
        ),
        scratch_shapes=[
            pltpu.VMEM((lines, LANES), jnp.float32),
            pltpu.VMEM((2 * LANES, lines), jnp.bfloat16),
            pltpu.VMEM((3 * list_lines, LANES), jnp.float32),
        ],
        compiler_params=pltpu.CompilerParams(vmem_limit_bytes=VMEM_LIMIT),
    )(wanted.reshape(steps, span))
    overflow = jnp.max(highest) > capacity
    return lists.reshape(members, capacity), place.reshape(-1), overflow


def around(array, axis):
    size = lax.axis_size(axis)
    return [array] + [
        lax.ppermute(array, axis, [(i, (i + d) % size) for i in range(size)])
        for d in range(1, size)
    ]


def body(queries, centroids, doc_resid, doc_codes, doc_scale, doc_len, send_list, cand):
    groups = lax.axis_size("group")
    members = lax.axis_size("member")
    capacity_sent = send_list.shape[2]
    block, width = doc_resid.shape[1:]
    shard = centroids.shape[0]
    qcount, qtokens = queries.shape[:2]

    chosen = send_list[0].reshape(-1)
    slots = chosen.shape[0]
    codes = jnp.take(doc_codes, chosen, axis=0)
    scales = jnp.take(doc_scale, chosen, axis=0).astype(jnp.float32)
    lengths = jnp.take(doc_len, chosen, axis=0)
    valid = jnp.arange(block, dtype=jnp.int32)[None, :] < lengths[:, None]

    lookups = slots * block
    capacity = -(-lookups // (2 * members * LANES)) * LANES
    lists, place, overflow = make_lists(jnp.where(valid, codes, -1), members, shard, capacity)
    flag = jnp.broadcast_to(overflow.astype(jnp.int32), (members, LANES))
    asked = lax.all_to_all(
        jnp.concatenate([lists, flag], axis=1), "member", split_axis=0, concat_axis=0, tiled=True
    )
    overflow = jnp.max(asked[:, capacity:]) > 0
    rows = fetch_rows(asked[:, :capacity].reshape(-1), centroids)
    received = lax.all_to_all(rows, "member", split_axis=0, concat_axis=0, tiled=True)

    turned = queries.transpose(2, 1, 0).reshape(width, qtokens * qcount)
    every_query = jnp.stack(around(turned, "group"))
    me = lax.axis_index("group")
    holder = lax.rem(me - jnp.arange(groups, dtype=jnp.int32) + groups, groups)

    def listed():
        return score(
            chosen, place, lengths, scales, holder, received, doc_resid, every_query, qcount
        )

    def whole_table():
        copies = jnp.broadcast_to(centroids[None], (members, shard, width))
        table = lax.all_to_all(copies, "member", split_axis=0, concat_axis=0, tiled=True)
        table = table.reshape(members * shard, width)
        base = jnp.take(table, codes.reshape(-1), axis=0)
        own = jnp.arange(lookups, dtype=jnp.int32)
        return score(
            chosen, own, lengths, scales, holder, base, doc_resid, every_query, qcount
        )

    local = lax.cond(overflow, whole_table, listed)
    local = local.reshape(groups * members, capacity_sent, qcount)
    returned = lax.all_to_all(local, ("group", "member"), split_axis=0, concat_axis=0, tiled=True)
    dense = returned.reshape(-1, qcount).T
    hit = cand[:, :, None] == jnp.arange(dense.shape[1], dtype=jnp.int32)
    return jnp.sum(jnp.where(hit, dense[:, None, :], 0.0), axis=2)


def solution(mesh):
    placed = (
        P("group", None, None),
        P("member", None),
        P(("group", "member"), None, None),
        P(("group", "member"), None),
        P(("group", "member")),
        P(("group", "member")),
        P(("group", "member"), None, None),
        P("group", "member"),
    )
    return jax.shard_map(
        body, mesh=mesh, in_specs=placed, out_specs=P("group", "member"), check_vma=False
    )
```

```python
import functools

import jax
import jax.numpy as jnp
from jax import lax
from jax.experimental import pallas as pl
from jax.experimental.pallas import tpu as pltpu
from jax.sharding import PartitionSpec as P

LANES = 128
GRAIN = 256
PAD = 8
VMEM_LIMIT = 56 * 1024 * 1024


def widen(source, wide, offset, rows):
    step = 256

    @pl.loop(0, rows // step)
    def _(i):
        at = pl.multiple_of(i * step, step)
        wide[pl.ds(at + offset, step), :] = source[pl.ds(at, step), :].astype(jnp.float32)


def fetch_kernel(entries, table, out, wide, stage):
    rows = table.shape[0]
    widen(table, wide, PAD, rows)
    block = stage.shape[0]

    @pl.loop(0, out.shape[0] // block)
    def _(b):
        at = pl.multiple_of(b * block, block)

        @pl.when(entries[at] > 0)
        def _():
            for u in range(block):
                stage[pl.ds(u, 1), :] = wide[pl.ds(entries[at + u], 1), :]
            out[pl.ds(at, block), :] = stage[...].astype(out.dtype)


def fetch_rows(entries, table):
    count, (rows, width) = entries.shape[0], table.shape
    return pl.pallas_call(
        fetch_kernel,
        out_shape=jax.ShapeDtypeStruct((count, width), table.dtype),
        grid_spec=pltpu.PrefetchScalarGridSpec(
            num_scalar_prefetch=1,
            grid=(1,),
            in_specs=[pl.BlockSpec((rows, width), lambda i, e: (0, 0))],
            out_specs=pl.BlockSpec((count, width), lambda i, e: (0, 0)),
            scratch_shapes=[
                pltpu.VMEM((rows + PAD, width), jnp.float32),
                pltpu.VMEM((LANES, width), jnp.float32),
            ],
        ),
        compiler_params=pltpu.CompilerParams(vmem_limit_bytes=VMEM_LIMIT),
    )(entries, table)


def score_kernel(docs, qtokens, chosen, place, lengths, scales, holder, received, *refs):
    residuals, (queries, out, wide, stage, embedded) = refs[:docs], refs[docs:]
    step = pl.program_id(0)
    block, width = stage.shape
    tile = 16

    @pl.when(step == 0)
    def _():
        widen(received, wide, 0, received.shape[0])

    slot = lax.broadcasted_iota(jnp.int32, (block, width), 0)
    for k in range(docs):
        doc = step * docs + k
        length = lengths[doc]
        base = doc * block
        for first in range(0, block, tile):

            @pl.when(first < length)
            def _():
                for u in range(first, first + tile):
                    stage[pl.ds(u, 1), :] = wide[pl.ds(place[base + u], 1), :]

        value = stage[...] + scales[doc] * residuals[k][0].astype(jnp.float32)
        value = jnp.where(slot < length, value, value[0:1, :])
        embedded[pl.ds(k * block, block), :] = value.astype(embedded.dtype)

    chunk = out.shape[1]
    total = jnp.zeros(out.shape, jnp.float32)
    for first in range(0, queries.shape[1], chunk):
        sims = lax.dot_general(
            embedded[...],
            queries[0, first : first + chunk, :],
            (((1,), (1,)), ((), ())),
            preferred_element_type=jnp.float32,
        )
        total = total + jnp.max(sims.reshape(docs, block, chunk), axis=1)
    out[...] = total * (1.0 / qtokens)


def score(chosen, place, lengths, scales, holder, received, doc_resid, queries, qcount):
    slots = chosen.shape[0]
    block, width = doc_resid.shape[1:]
    groups, columns, _ = queries.shape
    docs = 8
    per_group = slots // groups
    chunk = max(256, qcount)

    def residual_spec(k):
        return pl.BlockSpec(
            (1, block, width), lambda i, chosen, *_: (chosen[i * docs + k], 0, 0)
        )

    out = pl.pallas_call(
        functools.partial(score_kernel, docs, columns // qcount),
        out_shape=jax.ShapeDtypeStruct((slots, chunk), jnp.float32),
        grid_spec=pltpu.PrefetchScalarGridSpec(
            num_scalar_prefetch=5,
            grid=(slots // docs,),
            in_specs=[pl.BlockSpec(received.shape, lambda i, *_: (0, 0))]
            + [residual_spec(k) for k in range(docs)]
            + [
                pl.BlockSpec(
                    (1, columns, width),
                    lambda i, chosen, place, lengths, scales, holder, *_: (
                        holder[i * docs // per_group],
                        0,
                        0,
                    ),
                )
            ],
            out_specs=pl.BlockSpec((docs, chunk), lambda i, *_: (i, 0)),
            scratch_shapes=[
                pltpu.VMEM(received.shape, jnp.float32),
                pltpu.VMEM((block, width), jnp.float32),
                pltpu.VMEM((docs * block, width), jnp.bfloat16),
            ],
        ),
        compiler_params=pltpu.CompilerParams(vmem_limit_bytes=VMEM_LIMIT),
    )(chosen, place, lengths, scales, holder, received, *([doc_resid] * docs), queries)
    return out.reshape(slots, chunk // qcount, qcount).sum(axis=1)


def pack_kernel(members, capacity, codes, place, lists, highest, seen, whole, ranks, sums):
    steps, span = codes.shape
    lines = seen.shape[0]
    part = lines // members
    shard = part * GRAIN
    stripe = min(256, lines)
    bits = GRAIN.bit_length() - 1
    list_lines = lists.shape[0]

    def same(count, row, first=0):
        row = jnp.broadcast_to((row - first).astype(jnp.float32), (16, span))
        row = row.astype(jnp.bfloat16)[None]
        index = lax.broadcasted_iota(jnp.int32, (count, span), 0).astype(jnp.float32)
        index = index.astype(jnp.bfloat16).reshape(count // 16, 16, span)
        one, zero = jnp.ones((), jnp.bfloat16), jnp.zeros((), jnp.bfloat16)
        return jnp.where(index == row, one, zero).reshape(count, span)

    def across(left, right):
        return lax.dot_general(
            left, right, (((1,), (1,)), ((), ())), preferred_element_type=jnp.float32
        )

    seen[...] = jnp.zeros_like(seen)
    sums[...] = jnp.zeros_like(sums)

    @pl.loop(0, steps, unroll=4)
    def _(i):
        code = codes[pl.ds(i, 1), :]
        line, lane = code >> bits, code & (GRAIN - 1)
        right = same(GRAIN, lane)
        for first in range(0, lines, stripe):
            seen[first : first + stripe, :] += across(same(stripe, line, first), right)

    square = (GRAIN, GRAIN)
    earlier_lane = lax.broadcasted_iota(jnp.int32, square, 0) < lax.broadcasted_iota(
        jnp.int32, square, 1
    )
    earlier_lane = jnp.where(earlier_lane, 1.0, 0.0).astype(jnp.bfloat16)
    every_lane = jnp.ones(square, jnp.bfloat16)
    square = (part, part)
    earlier_line = lax.broadcasted_iota(jnp.int32, square, 1) < lax.broadcasted_iota(
        jnp.int32, square, 0
    )
    earlier_line = jnp.where(earlier_line, 1.0, 0.0).astype(jnp.bfloat16)
    top = jnp.zeros((1, GRAIN), jnp.float32)
    for o in range(members):
        at = slice(o * part, (o + 1) * part)
        present = jnp.where(seen[at, :] > 0.0, 1.0, 0.0)
        marks = present.astype(jnp.bfloat16)
        above = jnp.dot(earlier_line, marks, preferred_element_type=jnp.float32)
        rank = jnp.dot(marks, earlier_lane, preferred_element_type=jnp.float32) + jnp.dot(
            above.astype(jnp.bfloat16), every_lane, preferred_element_type=jnp.float32
        )
        top = jnp.maximum(top, jnp.max(present * (rank + 1.0), axis=0, keepdims=True))
        coarse = jnp.floor(rank * (1.0 / LANES))
        fine = rank - coarse * LANES
        whole[at, :] = jnp.concatenate([coarse, fine], axis=1)
    highest[...] = jnp.broadcast_to(top, highest.shape)
    ranks[...] = whole[...].T.astype(jnp.bfloat16)

    @pl.loop(0, steps, unroll=4)
    def _(i):
        code = codes[pl.ds(i, 1), :]
        line, lane = code >> bits, code & (GRAIN - 1)
        found = jnp.zeros((2 * GRAIN, span), jnp.float32)
        for first in range(0, lines, stripe):
            found += jnp.dot(
                ranks[:, first : first + stripe],
                same(stripe, line, first),
                preferred_element_type=jnp.float32,
            )
        mine = lax.broadcasted_iota(jnp.int32, (GRAIN, span), 0) == lane
        pick = jnp.where(mine, found[:GRAIN] * LANES + found[GRAIN:], 0.0)
        rank = jnp.sum(pick, axis=0, keepdims=True).astype(jnp.int32)
        held = (code >= 0) & (rank < capacity)
        owner = jnp.maximum(line, 0) // part
        spot = jnp.where(held, owner * capacity + rank, 0)
        place[pl.ds(i, 1), :] = spot
        entry = code - owner * shard + PAD
        mark = same(list_lines, jnp.where(held, spot >> 7, -1)).astype(jnp.float32)
        left = jnp.concatenate(
            [
                mark * (entry & 255).astype(jnp.float32),
                mark * (entry >> 8).astype(jnp.float32),
                mark,
            ],
            axis=0,
        )
        sums[...] += across(left.astype(jnp.bfloat16), same(LANES, spot & (LANES - 1)))

    times = jnp.maximum(sums[2 * list_lines :, :], 1.0)
    low = (sums[:list_lines, :] / times + 0.5).astype(jnp.int32)
    high = (sums[list_lines : 2 * list_lines, :] / times + 0.5).astype(jnp.int32)
    lists[...] = low + 256 * high


def make_lists(wanted, members, shard, capacity):
    span = 256
    steps = wanted.size // span
    lines = members * shard // GRAIN
    list_lines = members * capacity // LANES
    place, lists, highest = pl.pallas_call(
        functools.partial(pack_kernel, members, capacity),
        out_shape=(
            jax.ShapeDtypeStruct((steps, span), jnp.int32),
            jax.ShapeDtypeStruct((list_lines, LANES), jnp.int32),
            jax.ShapeDtypeStruct((8, GRAIN), jnp.float32),
        ),
        scratch_shapes=[
            pltpu.VMEM((lines, GRAIN), jnp.float32),
            pltpu.VMEM((lines, 2 * GRAIN), jnp.float32),
            pltpu.VMEM((2 * GRAIN, lines), jnp.bfloat16),
            pltpu.VMEM((3 * list_lines, LANES), jnp.float32),
        ],
        cost_estimate=pl.CostEstimate(
            flops=24 * wanted.size * lines * GRAIN, bytes_accessed=12 * wanted.size, transcendentals=0
        ),
        compiler_params=pltpu.CompilerParams(vmem_limit_bytes=VMEM_LIMIT),
    )(wanted.reshape(steps, span))
    overflow = jnp.max(highest) > capacity
    return lists.reshape(members, capacity), place.reshape(-1), overflow


def around(array, axis):
    size = lax.axis_size(axis)
    return [array] + [
        lax.ppermute(array, axis, [(i, (i + d) % size) for i in range(size)])
        for d in range(1, size)
    ]


def body(queries, centroids, doc_resid, doc_codes, doc_scale, doc_len, send_list, cand):
    groups = lax.axis_size("group")
    members = lax.axis_size("member")
    capacity_sent = send_list.shape[2]
    block, width = doc_resid.shape[1:]
    shard = centroids.shape[0]
    qcount, qtokens = queries.shape[:2]

    turned = queries.transpose(1, 0, 2).reshape(qtokens * qcount, width)
    every_query = jnp.stack(around(turned, "group"))
    chosen = send_list[0].reshape(-1)
    slots = chosen.shape[0]
    codes = jnp.take(doc_codes, chosen, axis=0)
    scales = jnp.take(doc_scale, chosen, axis=0).astype(jnp.float32)
    lengths = jnp.take(doc_len, chosen, axis=0)
    valid = jnp.arange(block, dtype=jnp.int32)[None, :] < lengths[:, None]

    lookups = slots * block
    capacity = -(-lookups // (2 * members * LANES)) * LANES
    lists, place, overflow = make_lists(jnp.where(valid, codes, -1), members, shard, capacity)
    flag = jnp.broadcast_to(overflow.astype(jnp.int32), (members, LANES))
    asked = lax.all_to_all(
        jnp.concatenate([lists, flag], axis=1), "member", split_axis=0, concat_axis=0, tiled=True
    )
    asked, every_query = lax.optimization_barrier((asked, every_query))
    overflow = jnp.max(asked[:, capacity:]) > 0
    rows = fetch_rows(asked[:, :capacity].reshape(-1), centroids)
    received = lax.all_to_all(rows, "member", split_axis=0, concat_axis=0, tiled=True)

    me = lax.axis_index("group")
    holder = lax.rem(me - jnp.arange(groups, dtype=jnp.int32) + groups, groups)

    def listed():
        return score(
            chosen, place, lengths, scales, holder, received, doc_resid, every_query, qcount
        )

    def whole_table():
        copies = jnp.broadcast_to(centroids[None], (members, shard, width))
        table = lax.all_to_all(copies, "member", split_axis=0, concat_axis=0, tiled=True)
        table = table.reshape(members * shard, width)
        base = jnp.take(table, codes.reshape(-1), axis=0)
        own = jnp.arange(lookups, dtype=jnp.int32)
        return score(
            chosen, own, lengths, scales, holder, base, doc_resid, every_query, qcount
        )

    local = lax.cond(overflow, whole_table, listed)
    local = local.reshape(groups * members, capacity_sent, qcount)
    returned = lax.all_to_all(local, ("group", "member"), split_axis=0, concat_axis=0, tiled=True)
    dense = returned.reshape(-1, qcount).T
    hit = cand[:, :, None] == jnp.arange(dense.shape[1], dtype=jnp.int32)
    return jnp.sum(jnp.where(hit, dense[:, None, :], 0.0), axis=2)


def solution(mesh):
    placed = (
        P("group", None, None),
        P("member", None),
        P(("group", "member"), None, None),
        P(("group", "member"), None),
        P(("group", "member")),
        P(("group", "member")),
        P(("group", "member"), None, None),
        P("group", "member"),
    )
    return jax.shard_map(
        body, mesh=mesh, in_specs=placed, out_specs=P("group", "member"), check_vma=False
    )
```

```python
import functools

import jax
import jax.numpy as jnp
from jax import lax
from jax.experimental import pallas as pl
from jax.experimental.pallas import tpu as pltpu
from jax.sharding import PartitionSpec as P

LANES = 128
GRAIN = 256
PAD = 8
VMEM_LIMIT = 56 * 1024 * 1024


def widen(source, wide, offset, rows):
    step = 256

    @pl.loop(0, rows // step)
    def _(i):
        at = pl.multiple_of(i * step, step)
        wide[pl.ds(at + offset, step), :] = source[pl.ds(at, step), :].astype(jnp.float32)


def fetch_kernel(entries, table, out, wide, stage):
    rows = table.shape[0]
    widen(table, wide, PAD, rows)
    block = stage.shape[0]

    @pl.loop(0, out.shape[0] // block)
    def _(b):
        at = pl.multiple_of(b * block, block)

        @pl.when(entries[at] > 0)
        def _():
            for u in range(block):
                stage[pl.ds(u, 1), :] = wide[pl.ds(entries[at + u], 1), :]
            out[pl.ds(at, block), :] = stage[...].astype(out.dtype)


def fetch_rows(entries, table):
    count, (rows, width) = entries.shape[0], table.shape
    return pl.pallas_call(
        fetch_kernel,
        out_shape=jax.ShapeDtypeStruct((count, width), table.dtype),
        grid_spec=pltpu.PrefetchScalarGridSpec(
            num_scalar_prefetch=1,
            grid=(1,),
            in_specs=[pl.BlockSpec((rows, width), lambda i, e: (0, 0))],
            out_specs=pl.BlockSpec((count, width), lambda i, e: (0, 0)),
            scratch_shapes=[
                pltpu.VMEM((rows + PAD, width), jnp.float32),
                pltpu.VMEM((LANES, width), jnp.float32),
            ],
        ),
        compiler_params=pltpu.CompilerParams(vmem_limit_bytes=VMEM_LIMIT),
    )(entries, table)


def score_kernel(docs, qtokens, chosen, place, lengths, scales, holder, received, *refs):
    residuals, (queries, out, wide, stage, embedded) = refs[:docs], refs[docs:]
    step = pl.program_id(0)
    block, width = stage.shape
    tile = 16

    @pl.when(step == 0)
    def _():
        widen(received, wide, 0, received.shape[0])

    slot = lax.broadcasted_iota(jnp.int32, (block, width), 0)
    for k in range(docs):
        doc = step * docs + k
        length = lengths[doc]
        base = doc * block
        for first in range(0, block, tile):

            @pl.when(first < length)
            def _():
                for u in range(first, first + tile):
                    stage[pl.ds(u, 1), :] = wide[pl.ds(place[base + u], 1), :]

        value = stage[...] + scales[doc] * residuals[k][0].astype(jnp.float32)
        value = jnp.where(slot < length, value, value[0:1, :])
        embedded[pl.ds(k * block, block), :] = value.astype(embedded.dtype)

    chunk = out.shape[1]
    total = jnp.zeros(out.shape, jnp.float32)
    for first in range(0, queries.shape[1], chunk):
        sims = lax.dot_general(
            embedded[...],
            queries[0, first : first + chunk, :],
            (((1,), (1,)), ((), ())),
            preferred_element_type=jnp.float32,
        )
        total = total + jnp.max(sims.reshape(docs, block, chunk), axis=1)
    out[...] = total * (1.0 / qtokens)


def score(chosen, place, lengths, scales, holder, received, doc_resid, queries, qcount):
    slots = chosen.shape[0]
    block, width = doc_resid.shape[1:]
    groups, columns, _ = queries.shape
    docs = 8
    per_group = slots // groups
    chunk = max(256, qcount)

    def residual_spec(k):
        return pl.BlockSpec(
            (1, block, width), lambda i, chosen, *_: (chosen[i * docs + k], 0, 0)
        )

    out = pl.pallas_call(
        functools.partial(score_kernel, docs, columns // qcount),
        out_shape=jax.ShapeDtypeStruct((slots, chunk), jnp.float32),
        grid_spec=pltpu.PrefetchScalarGridSpec(
            num_scalar_prefetch=5,
            grid=(slots // docs,),
            in_specs=[pl.BlockSpec(received.shape, lambda i, *_: (0, 0))]
            + [residual_spec(k) for k in range(docs)]
            + [
                pl.BlockSpec(
                    (1, columns, width),
                    lambda i, chosen, place, lengths, scales, holder, *_: (
                        holder[i * docs // per_group],
                        0,
                        0,
                    ),
                )
            ],
            out_specs=pl.BlockSpec((docs, chunk), lambda i, *_: (i, 0)),
            scratch_shapes=[
                pltpu.VMEM(received.shape, jnp.float32),
                pltpu.VMEM((block, width), jnp.float32),
                pltpu.VMEM((docs * block, width), jnp.bfloat16),
            ],
        ),
        compiler_params=pltpu.CompilerParams(vmem_limit_bytes=VMEM_LIMIT),
    )(chosen, place, lengths, scales, holder, received, *([doc_resid] * docs), queries)
    return out.reshape(slots, chunk // qcount, qcount).sum(axis=1)


def exchange_kernel(axes, sizes, given, taken, send_sem, recv_sem):
    count = given.shape[0]
    me = jnp.int32(0)
    for axis, size in zip(axes, sizes):
        me = me * size + lax.axis_index(axis)

    def device(peer):
        where = {}
        for axis, size in reversed(list(zip(axes, sizes))):
            where[axis] = lax.rem(peer, size)
            peer = peer // size
        return where

    def at_distance(d):
        return lax.rem(me + d, count)

    barrier = pltpu.get_barrier_semaphore()
    for d in range(1, count):
        pl.semaphore_signal(
            barrier,
            inc=1,
            device_id=device(at_distance(d)),
            device_id_type=pl.DeviceIdType.MESH,
        )
    taken[me] = given[me]
    pl.semaphore_wait(barrier, count - 1)
    copies = []
    for d in range(1, count):
        peer = at_distance(d)
        copy = pltpu.make_async_remote_copy(
            src_ref=given.at[peer],
            dst_ref=taken.at[me],
            send_sem=send_sem.at[d],
            recv_sem=recv_sem.at[d],
            device_id=device(peer),
            device_id_type=pl.DeviceIdType.MESH,
        )
        copy.start()
        copies.append(copy)
    for copy in copies:
        copy.wait()


def exchange(given, axes, collective_id):
    sizes = tuple(lax.axis_size(axis) for axis in axes)
    count = given.shape[0]
    return pl.pallas_call(
        functools.partial(exchange_kernel, axes, sizes),
        out_shape=jax.ShapeDtypeStruct(given.shape, given.dtype),
        in_specs=[pl.BlockSpec(memory_space=pltpu.VMEM)],
        out_specs=pl.BlockSpec(memory_space=pltpu.VMEM),
        scratch_shapes=[
            pltpu.SemaphoreType.DMA((count,)),
            pltpu.SemaphoreType.DMA((count,)),
        ],
        compiler_params=pltpu.CompilerParams(
            collective_id=collective_id, has_side_effects=True
        ),
    )(given)


def pack_kernel(members, capacity, codes, place, lists, seen, whole, ranks, sums):
    steps, span = codes.shape
    lines = seen.shape[0]
    part = lines // members
    shard = part * GRAIN
    stripe = min(256, lines)
    bits = GRAIN.bit_length() - 1
    list_lines = members * capacity // LANES

    def same(count, row, first=0):
        row = jnp.broadcast_to((row - first).astype(jnp.float32), (16, span))
        row = row.astype(jnp.bfloat16)[None]
        index = lax.broadcasted_iota(jnp.int32, (count, span), 0).astype(jnp.float32)
        index = index.astype(jnp.bfloat16).reshape(count // 16, 16, span)
        one, zero = jnp.ones((), jnp.bfloat16), jnp.zeros((), jnp.bfloat16)
        return jnp.where(index == row, one, zero).reshape(count, span)

    def across(left, right):
        return lax.dot_general(
            left, right, (((1,), (1,)), ((), ())), preferred_element_type=jnp.float32
        )

    seen[...] = jnp.zeros_like(seen)
    sums[...] = jnp.zeros_like(sums)

    @pl.loop(0, steps, unroll=4)
    def _(i):
        code = codes[pl.ds(i, 1), :]
        line, lane = code >> bits, code & (GRAIN - 1)
        right = same(GRAIN, lane)
        for first in range(0, lines, stripe):
            seen[first : first + stripe, :] += across(same(stripe, line, first), right)

    square = (GRAIN, GRAIN)
    earlier_lane = lax.broadcasted_iota(jnp.int32, square, 0) < lax.broadcasted_iota(
        jnp.int32, square, 1
    )
    earlier_lane = jnp.where(earlier_lane, 1.0, 0.0).astype(jnp.bfloat16)
    every_lane = jnp.ones(square, jnp.bfloat16)
    square = (part, part)
    earlier_line = lax.broadcasted_iota(jnp.int32, square, 1) < lax.broadcasted_iota(
        jnp.int32, square, 0
    )
    earlier_line = jnp.where(earlier_line, 1.0, 0.0).astype(jnp.bfloat16)
    top = jnp.zeros((1, GRAIN), jnp.float32)
    for o in range(members):
        at = slice(o * part, (o + 1) * part)
        present = jnp.where(seen[at, :] > 0.0, 1.0, 0.0)
        marks = present.astype(jnp.bfloat16)
        above = jnp.dot(earlier_line, marks, preferred_element_type=jnp.float32)
        rank = jnp.dot(marks, earlier_lane, preferred_element_type=jnp.float32) + jnp.dot(
            above.astype(jnp.bfloat16), every_lane, preferred_element_type=jnp.float32
        )
        top = jnp.maximum(top, jnp.max(present * (rank + 1.0), axis=0, keepdims=True))
        coarse = jnp.floor(rank * (1.0 / LANES))
        fine = rank - coarse * LANES
        whole[at, :] = jnp.concatenate([coarse, fine], axis=1)
    top = jnp.max(top, axis=1, keepdims=True).astype(jnp.int32)
    ranks[...] = whole[...].T.astype(jnp.bfloat16)

    @pl.loop(0, steps, unroll=4)
    def _(i):
        code = codes[pl.ds(i, 1), :]
        line, lane = code >> bits, code & (GRAIN - 1)
        found = jnp.zeros((2 * GRAIN, span), jnp.float32)
        for first in range(0, lines, stripe):
            found += jnp.dot(
                ranks[:, first : first + stripe],
                same(stripe, line, first),
                preferred_element_type=jnp.float32,
            )
        mine = lax.broadcasted_iota(jnp.int32, (GRAIN, span), 0) == lane
        pick = jnp.where(mine, found[:GRAIN] * LANES + found[GRAIN:], 0.0)
        rank = jnp.sum(pick, axis=0, keepdims=True).astype(jnp.int32)
        held = (code >= 0) & (rank < capacity)
        owner = jnp.maximum(line, 0) // part
        spot = jnp.where(held, owner * capacity + rank, 0)
        place[pl.ds(i, 1), :] = spot
        entry = code - owner * shard + PAD
        mark = same(list_lines, jnp.where(held, spot >> 7, -1)).astype(jnp.float32)
        left = jnp.concatenate(
            [
                mark * (entry & 255).astype(jnp.float32),
                mark * (entry >> 8).astype(jnp.float32),
                mark,
            ],
            axis=0,
        )
        sums[...] += across(left.astype(jnp.bfloat16), same(LANES, spot & (LANES - 1)))

    times = jnp.maximum(sums[2 * list_lines :, :], 1.0)
    low = (sums[:list_lines, :] / times + 0.5).astype(jnp.int32)
    high = (sums[list_lines : 2 * list_lines, :] / times + 0.5).astype(jnp.int32)
    packed = low + 256 * high
    own = capacity // LANES
    for o in range(members):
        lists[o, 0:own, :] = packed[o * own : (o + 1) * own, :]
        lists[o, own:, :] = jnp.broadcast_to(top, (lists.shape[1] - own, LANES))


def make_lists(wanted, members, shard, capacity):
    span = 256
    steps = wanted.size // span
    lines = members * shard // GRAIN
    list_lines = members * capacity // LANES
    deep = (capacity // LANES // 8 + 1) * 8
    place, lists = pl.pallas_call(
        functools.partial(pack_kernel, members, capacity),
        out_shape=(
            jax.ShapeDtypeStruct((steps, span), jnp.int32),
            jax.ShapeDtypeStruct((members, deep, LANES), jnp.int32),
        ),
        scratch_shapes=[
            pltpu.VMEM((lines, GRAIN), jnp.float32),
            pltpu.VMEM((lines, 2 * GRAIN), jnp.float32),
            pltpu.VMEM((2 * GRAIN, lines), jnp.bfloat16),
            pltpu.VMEM((3 * list_lines, LANES), jnp.float32),
        ],
        cost_estimate=pl.CostEstimate(
            flops=24 * wanted.size * lines * GRAIN, bytes_accessed=12 * wanted.size, transcendentals=0
        ),
        compiler_params=pltpu.CompilerParams(vmem_limit_bytes=VMEM_LIMIT),
    )(wanted.reshape(steps, span))
    return lists, place.reshape(-1)


def around(array, axis):
    size = lax.axis_size(axis)
    return [array] + [
        lax.ppermute(array, axis, [(i, (i + d) % size) for i in range(size)])
        for d in range(1, size)
    ]


def body(queries, centroids, doc_resid, doc_codes, doc_scale, doc_len, send_list, cand):
    groups = lax.axis_size("group")
    members = lax.axis_size("member")
    capacity_sent = send_list.shape[2]
    block, width = doc_resid.shape[1:]
    shard = centroids.shape[0]
    qcount, qtokens = queries.shape[:2]

    turned = queries.transpose(1, 0, 2).reshape(qtokens * qcount, width)
    every_query = jnp.stack(around(turned, "group"))
    chosen = send_list[0].reshape(-1)
    slots = chosen.shape[0]
    codes = jnp.take(doc_codes, chosen, axis=0)
    scales = jnp.take(doc_scale, chosen, axis=0).astype(jnp.float32)
    lengths = jnp.take(doc_len, chosen, axis=0)
    valid = jnp.arange(block, dtype=jnp.int32)[None, :] < lengths[:, None]

    lookups = slots * block
    capacity = -(-lookups // (2 * members * LANES)) * LANES
    lists, place = make_lists(jnp.where(valid, codes, -1), members, shard, capacity)
    asked = exchange(lists, ("member",), 0)
    asked, every_query = lax.optimization_barrier((asked, every_query))
    own = capacity // LANES
    overflow = jnp.max(asked[:, own]) > capacity
    rows = fetch_rows(asked[:, :own].reshape(-1), centroids)
    received = lax.all_to_all(rows, "member", split_axis=0, concat_axis=0, tiled=True)

    me = lax.axis_index("group")
    holder = lax.rem(me - jnp.arange(groups, dtype=jnp.int32) + groups, groups)

    def listed():
        return score(
            chosen, place, lengths, scales, holder, received, doc_resid, every_query, qcount
        )

    def whole_table():
        copies = jnp.broadcast_to(centroids[None], (members, shard, width))
        table = lax.all_to_all(copies, "member", split_axis=0, concat_axis=0, tiled=True)
        table = table.reshape(members * shard, width)
        base = jnp.take(table, codes.reshape(-1), axis=0)
        own = jnp.arange(lookups, dtype=jnp.int32)
        return score(
            chosen, own, lengths, scales, holder, base, doc_resid, every_query, qcount
        )

    local = lax.cond(overflow, whole_table, listed)
    local = local.reshape(groups * members, capacity_sent, qcount)
    returned = lax.all_to_all(local, ("group", "member"), split_axis=0, concat_axis=0, tiled=True)
    dense = returned.reshape(-1, qcount).T
    hit = cand[:, :, None] == jnp.arange(dense.shape[1], dtype=jnp.int32)
    return jnp.sum(jnp.where(hit, dense[:, None, :], 0.0), axis=2)


def solution(mesh):
    placed = (
        P("group", None, None),
        P("member", None),
        P(("group", "member"), None, None),
        P(("group", "member"), None),
        P(("group", "member")),
        P(("group", "member")),
        P(("group", "member"), None, None),
        P("group", "member"),
    )
    return jax.shard_map(
        body, mesh=mesh, in_specs=placed, out_specs=P("group", "member"), check_vma=False
    )
```

```python
import functools

import jax
import jax.numpy as jnp
from jax import lax
from jax.experimental import pallas as pl
from jax.experimental.pallas import tpu as pltpu
from jax.sharding import PartitionSpec as P

LANES = 128
GRAIN = 256
PAD = 8
VMEM_LIMIT = 56 * 1024 * 1024


def widen(source, wide, offset, rows):
    step = 256

    @pl.loop(0, rows // step)
    def _(i):
        at = pl.multiple_of(i * step, step)
        wide[pl.ds(at + offset, step), :] = source[pl.ds(at, step), :].astype(jnp.float32)


def fetch_kernel(entries, table, out, wide, stage):
    rows = table.shape[0]
    widen(table, wide, PAD, rows)
    block = stage.shape[0]

    @pl.loop(0, out.shape[0] // block)
    def _(b):
        at = pl.multiple_of(b * block, block)

        @pl.when(entries[at] > 0)
        def _():
            for u in range(block):
                stage[pl.ds(u, 1), :] = wide[pl.ds(entries[at + u], 1), :]
            out[pl.ds(at, block), :] = stage[...].astype(out.dtype)


def fetch_rows(entries, table):
    count, (rows, width) = entries.shape[0], table.shape
    return pl.pallas_call(
        fetch_kernel,
        out_shape=jax.ShapeDtypeStruct((count, width), table.dtype),
        grid_spec=pltpu.PrefetchScalarGridSpec(
            num_scalar_prefetch=1,
            grid=(1,),
            in_specs=[pl.BlockSpec((rows, width), lambda i, e: (0, 0))],
            out_specs=pl.BlockSpec((count, width), lambda i, e: (0, 0)),
            scratch_shapes=[
                pltpu.VMEM((rows + PAD, width), jnp.float32),
                pltpu.VMEM((LANES, width), jnp.float32),
            ],
        ),
        compiler_params=pltpu.CompilerParams(vmem_limit_bytes=VMEM_LIMIT),
    )(entries, table)


def score_kernel(docs, qtokens, chosen, place, lengths, scales, holder, received, *refs):
    residuals, (queries, out, wide, stage, embedded) = refs[:docs], refs[docs:]
    step = pl.program_id(0)
    block, width = stage.shape
    tile = 16

    @pl.when(step == 0)
    def _():
        widen(received, wide, 0, received.shape[0])

    slot = lax.broadcasted_iota(jnp.int32, (block, width), 0)
    for k in range(docs):
        doc = step * docs + k
        length = lengths[doc]
        base = doc * block
        for first in range(0, block, tile):

            @pl.when(first < length)
            def _():
                for u in range(first, first + tile):
                    stage[pl.ds(u, 1), :] = wide[pl.ds(place[base + u], 1), :]

        value = stage[...] + scales[doc] * residuals[k][0].astype(jnp.float32)
        value = jnp.where(slot < length, value, value[0:1, :])
        embedded[pl.ds(k * block, block), :] = value.astype(embedded.dtype)

    chunk = out.shape[1]
    total = jnp.zeros(out.shape, jnp.float32)
    for first in range(0, queries.shape[1], chunk):
        sims = lax.dot_general(
            embedded[...],
            queries[0, first : first + chunk, :],
            (((1,), (1,)), ((), ())),
            preferred_element_type=jnp.float32,
        )
        total = total + jnp.max(sims.reshape(docs, block, chunk), axis=1)
    out[...] = total * (1.0 / qtokens)


def score(chosen, place, lengths, scales, holder, received, doc_resid, queries, qcount):
    slots = chosen.shape[0]
    block, width = doc_resid.shape[1:]
    groups, columns, _ = queries.shape
    docs = 8
    per_group = slots // groups
    chunk = max(256, qcount)

    def residual_spec(k):
        return pl.BlockSpec(
            (1, block, width), lambda i, chosen, *_: (chosen[i * docs + k], 0, 0)
        )

    out = pl.pallas_call(
        functools.partial(score_kernel, docs, columns // qcount),
        out_shape=jax.ShapeDtypeStruct((slots, chunk), jnp.float32),
        grid_spec=pltpu.PrefetchScalarGridSpec(
            num_scalar_prefetch=5,
            grid=(slots // docs,),
            in_specs=[pl.BlockSpec(received.shape, lambda i, *_: (0, 0))]
            + [residual_spec(k) for k in range(docs)]
            + [
                pl.BlockSpec(
                    (1, columns, width),
                    lambda i, chosen, place, lengths, scales, holder, *_: (
                        holder[i * docs // per_group],
                        0,
                        0,
                    ),
                )
            ],
            out_specs=pl.BlockSpec((docs, chunk), lambda i, *_: (i, 0)),
            scratch_shapes=[
                pltpu.VMEM(received.shape, jnp.float32),
                pltpu.VMEM((block, width), jnp.float32),
                pltpu.VMEM((docs * block, width), jnp.bfloat16),
            ],
        ),
        compiler_params=pltpu.CompilerParams(vmem_limit_bytes=VMEM_LIMIT),
    )(chosen, place, lengths, scales, holder, received, *([doc_resid] * docs), queries)
    return out.reshape(slots, chunk // qcount, qcount).sum(axis=1)


def exchange_kernel(axes, sizes, given, taken, send_sem, recv_sem):
    count = given.shape[0]
    me = jnp.int32(0)
    for axis, size in zip(axes, sizes):
        me = me * size + lax.axis_index(axis)

    def device(peer):
        where = {}
        for axis, size in reversed(list(zip(axes, sizes))):
            where[axis] = lax.rem(peer, size)
            peer = peer // size
        return where

    def at_distance(d):
        return lax.rem(me + d, count)

    barrier = pltpu.get_barrier_semaphore()
    for d in range(1, count):
        pl.semaphore_signal(
            barrier,
            inc=1,
            device_id=device(at_distance(d)),
            device_id_type=pl.DeviceIdType.MESH,
        )
    taken[me] = given[me]
    pl.semaphore_wait(barrier, count - 1)
    copies = []
    for d in range(1, count):
        peer = at_distance(d)
        copy = pltpu.make_async_remote_copy(
            src_ref=given.at[peer],
            dst_ref=taken.at[me],
            send_sem=send_sem.at[d],
            recv_sem=recv_sem.at[d],
            device_id=device(peer),
            device_id_type=pl.DeviceIdType.MESH,
        )
        copy.start()
        copies.append(copy)
    for copy in copies:
        copy.wait()


def exchange(given, axes, collective_id):
    sizes = tuple(lax.axis_size(axis) for axis in axes)
    count = given.shape[0]
    return pl.pallas_call(
        functools.partial(exchange_kernel, axes, sizes),
        out_shape=jax.ShapeDtypeStruct(given.shape, given.dtype),
        in_specs=[pl.BlockSpec(memory_space=pltpu.VMEM)],
        out_specs=pl.BlockSpec(memory_space=pltpu.VMEM),
        scratch_shapes=[
            pltpu.SemaphoreType.DMA((count,)),
            pltpu.SemaphoreType.DMA((count,)),
        ],
        compiler_params=pltpu.CompilerParams(
            collective_id=collective_id, has_side_effects=True
        ),
    )(given)


def pack_kernel(members, capacity, codes, place, lists, seen, whole, ranks, sums):
    steps, span = codes.shape
    lines = seen.shape[0]
    part = lines // members
    shard = part * GRAIN
    stripe = min(256, lines)
    bits = GRAIN.bit_length() - 1
    list_lines = -(-members * capacity // LANES // 16) * 16

    def same(count, row, first=0):
        row = jnp.broadcast_to((row - first).astype(jnp.float32), (16, span))
        row = row.astype(jnp.bfloat16)[None]
        index = lax.broadcasted_iota(jnp.int32, (count, span), 0).astype(jnp.float32)
        index = index.astype(jnp.bfloat16).reshape(count // 16, 16, span)
        one, zero = jnp.ones((), jnp.bfloat16), jnp.zeros((), jnp.bfloat16)
        return jnp.where(index == row, one, zero).reshape(count, span)

    def across(left, right):
        return lax.dot_general(
            left, right, (((1,), (1,)), ((), ())), preferred_element_type=jnp.float32
        )

    seen[...] = jnp.zeros_like(seen)
    sums[...] = jnp.zeros_like(sums)

    @pl.loop(0, steps, unroll=4)
    def _(i):
        code = codes[pl.ds(i, 1), :]
        line, lane = code >> bits, code & (GRAIN - 1)
        right = same(GRAIN, lane)
        for first in range(0, lines, stripe):
            seen[first : first + stripe, :] += across(same(stripe, line, first), right)

    square = (GRAIN, GRAIN)
    earlier_lane = lax.broadcasted_iota(jnp.int32, square, 0) < lax.broadcasted_iota(
        jnp.int32, square, 1
    )
    earlier_lane = jnp.where(earlier_lane, 1.0, 0.0).astype(jnp.bfloat16)
    every_lane = jnp.ones(square, jnp.bfloat16)
    square = (part, part)
    earlier_line = lax.broadcasted_iota(jnp.int32, square, 1) < lax.broadcasted_iota(
        jnp.int32, square, 0
    )
    earlier_line = jnp.where(earlier_line, 1.0, 0.0).astype(jnp.bfloat16)
    top = jnp.zeros((1, GRAIN), jnp.float32)
    for o in range(members):
        at = slice(o * part, (o + 1) * part)
        present = jnp.where(seen[at, :] > 0.0, 1.0, 0.0)
        marks = present.astype(jnp.bfloat16)
        above = jnp.dot(earlier_line, marks, preferred_element_type=jnp.float32)
        rank = jnp.dot(marks, earlier_lane, preferred_element_type=jnp.float32) + jnp.dot(
            above.astype(jnp.bfloat16), every_lane, preferred_element_type=jnp.float32
        )
        top = jnp.maximum(top, jnp.max(present * (rank + 1.0), axis=0, keepdims=True))
        coarse = jnp.floor(rank * (1.0 / LANES))
        fine = rank - coarse * LANES
        whole[at, :] = jnp.concatenate([coarse, fine], axis=1)
    top = jnp.max(top, axis=1, keepdims=True).astype(jnp.int32)
    ranks[...] = whole[...].T.astype(jnp.bfloat16)

    @pl.loop(0, steps, unroll=4)
    def _(i):
        code = codes[pl.ds(i, 1), :]
        line, lane = code >> bits, code & (GRAIN - 1)
        found = jnp.zeros((2 * GRAIN, span), jnp.float32)
        for first in range(0, lines, stripe):
            found += jnp.dot(
                ranks[:, first : first + stripe],
                same(stripe, line, first),
                preferred_element_type=jnp.float32,
            )
        mine = lax.broadcasted_iota(jnp.int32, (GRAIN, span), 0) == lane
        pick = jnp.where(mine, found[:GRAIN] * LANES + found[GRAIN:], 0.0)
        rank = jnp.sum(pick, axis=0, keepdims=True).astype(jnp.int32)
        held = (code >= 0) & (rank < capacity)
        owner = jnp.maximum(line, 0) // part
        spot = jnp.where(held, owner * capacity + rank, 0)
        place[pl.ds(i, 1), :] = spot
        entry = code - owner * shard + PAD
        mark = same(list_lines, jnp.where(held, spot >> 7, -1)).astype(jnp.float32)
        left = jnp.concatenate(
            [
                mark * (entry & 255).astype(jnp.float32),
                mark * (entry >> 8).astype(jnp.float32),
                mark,
            ],
            axis=0,
        )
        sums[...] += across(left.astype(jnp.bfloat16), same(LANES, spot & (LANES - 1)))

    times = jnp.maximum(sums[2 * list_lines :, :], 1.0)
    low = (sums[:list_lines, :] / times + 0.5).astype(jnp.int32)
    high = (sums[list_lines : 2 * list_lines, :] / times + 0.5).astype(jnp.int32)
    packed = low + 256 * high
    own = capacity // LANES
    for o in range(members):
        lists[o, 0:own, :] = packed[o * own : (o + 1) * own, :]
        lists[o, own:, :] = jnp.broadcast_to(top, (lists.shape[1] - own, LANES))


def make_lists(wanted, members, shard, capacity):
    span = 256
    steps = wanted.size // span
    lines = members * shard // GRAIN
    list_lines = -(-members * capacity // LANES // 16) * 16
    deep = (capacity // LANES // 8 + 1) * 8
    place, lists = pl.pallas_call(
        functools.partial(pack_kernel, members, capacity),
        out_shape=(
            jax.ShapeDtypeStruct((steps, span), jnp.int32),
            jax.ShapeDtypeStruct((members, deep, LANES), jnp.int32),
        ),
        scratch_shapes=[
            pltpu.VMEM((lines, GRAIN), jnp.float32),
            pltpu.VMEM((lines, 2 * GRAIN), jnp.float32),
            pltpu.VMEM((2 * GRAIN, lines), jnp.bfloat16),
            pltpu.VMEM((3 * list_lines, LANES), jnp.float32),
        ],
        cost_estimate=pl.CostEstimate(
            flops=24 * wanted.size * lines * GRAIN, bytes_accessed=12 * wanted.size, transcendentals=0
        ),
        compiler_params=pltpu.CompilerParams(vmem_limit_bytes=VMEM_LIMIT),
    )(wanted.reshape(steps, span))
    return lists, place.reshape(-1)


def around(array, axis):
    size = lax.axis_size(axis)
    return [array] + [
        lax.ppermute(array, axis, [(i, (i + d) % size) for i in range(size)])
        for d in range(1, size)
    ]


def body(queries, centroids, doc_resid, doc_codes, doc_scale, doc_len, send_list, cand):
    groups = lax.axis_size("group")
    members = lax.axis_size("member")
    capacity_sent = send_list.shape[2]
    block, width = doc_resid.shape[1:]
    shard = centroids.shape[0]
    qcount, qtokens = queries.shape[:2]

    turned = queries.transpose(1, 0, 2).reshape(qtokens * qcount, width)
    every_query = jnp.stack(around(turned, "group"))
    chosen = send_list[0].reshape(-1)
    slots = chosen.shape[0]
    codes = jnp.take(doc_codes, chosen, axis=0)
    scales = jnp.take(doc_scale, chosen, axis=0).astype(jnp.float32)
    lengths = jnp.take(doc_len, chosen, axis=0)
    valid = jnp.arange(block, dtype=jnp.int32)[None, :] < lengths[:, None]

    lookups = slots * block
    capacity = -(-3 * lookups // (8 * members * LANES)) * LANES
    lists, place = make_lists(jnp.where(valid, codes, -1), members, shard, capacity)
    asked = exchange(lists, ("member",), 0)
    asked, every_query = lax.optimization_barrier((asked, every_query))
    own = capacity // LANES
    overflow = jnp.max(asked[:, own]) > capacity
    rows = fetch_rows(asked[:, :own].reshape(-1), centroids)
    received = lax.all_to_all(rows, "member", split_axis=0, concat_axis=0, tiled=True)

    me = lax.axis_index("group")
    holder = lax.rem(me - jnp.arange(groups, dtype=jnp.int32) + groups, groups)

    def listed():
        return score(
            chosen, place, lengths, scales, holder, received, doc_resid, every_query, qcount
        )

    def whole_table():
        copies = jnp.broadcast_to(centroids[None], (members, shard, width))
        table = lax.all_to_all(copies, "member", split_axis=0, concat_axis=0, tiled=True)
        table = table.reshape(members * shard, width)
        base = jnp.take(table, codes.reshape(-1), axis=0)
        own = jnp.arange(lookups, dtype=jnp.int32)
        return score(
            chosen, own, lengths, scales, holder, base, doc_resid, every_query, qcount
        )

    local = lax.cond(overflow, whole_table, listed)
    local = local.reshape(groups * members, 1, capacity_sent * qcount)
    returned = exchange(local, ("group", "member"), 1)
    dense = returned.reshape(-1, qcount).T
    hit = cand[:, :, None] == jnp.arange(dense.shape[1], dtype=jnp.int32)
    return jnp.sum(jnp.where(hit, dense[:, None, :], 0.0), axis=2)


def solution(mesh):
    placed = (
        P("group", None, None),
        P("member", None),
        P(("group", "member"), None, None),
        P(("group", "member"), None),
        P(("group", "member")),
        P(("group", "member")),
        P(("group", "member"), None, None),
        P("group", "member"),
    )
    return jax.shard_map(
        body, mesh=mesh, in_specs=placed, out_specs=P("group", "member"), check_vma=False
    )
```
